32 devices in a mesh: section: 16 (over z, y, x), head: 2 (over core).
Axes of the slice: x: 2, y: 2, z: 4, core: 2. Of those that a mesh axis runs over, the one named last changes fastest.
Arguments:
- queries: bfloat16 [3072, 1024], P('section', 'head'), may hold values from -20 to 20
- keys: bfloat16 [3072, 256], P('section', 'head'), may hold values from -20 to 20
- values: bfloat16 [3072, 256], P('section', 'head'), may hold values from -6 to 6
- d_attn: bfloat16 [3072, 1024], P('section', 'head'), may hold values from -72 to 72
- d_out: bfloat16 [3072, 4096], P('section', 'head'), may hold values from -6 to 6
- w_query: bfloat16 [4096, 1024], P(None, 'head'), may hold values from -0.09375 to 0.09375
- prefix_len: int32 [16], replicated, may hold values from 0 to 2880, as said below
Outputs:
- grad_prev: bfloat16 [3072, 4096], P('section', 'head')
The draws below stay inside these ranges and needn't reach their ends.
Inputs may be any that keep to these rules, and one draw needn't show every extreme that they name: prefix_len[s] <= s * 192 for every slice s; the first slice's is 0 and the last slice's is 2880.
All inputs are finite; a program needn't handle non-finite values.
Results may differ from the reference program's by a relative error of at most 0.035.
Values may be sent and summed in bfloat16 or wider, within the bound.
A program may use at most 64 MiB of HBM per device.

```python
import jax
import jax.numpy as jnp
from jax import lax

D = 4096
HEAD_DIM = 128
QH_DEV = 4
ROWS = 192
SLICES = 16
TOKENS = 3072
KV_HEADS = 2
QHEADS = 8
LMAX = 2880


def draw_queries(key, part):
    base_draw = jnp.clip(jax.random.normal(jax.random.fold_in(key, 11), (TOKENS, QHEADS * HEAD_DIM), jnp.float32), -5.0, 5.0)
    return base_draw.astype(jnp.bfloat16)


def draw_keys(key, part):
    base_draw = jnp.clip(jax.random.normal(jax.random.fold_in(key, 13), (TOKENS, KV_HEADS * HEAD_DIM), jnp.float32), -5.0, 5.0)
    return base_draw.astype(jnp.bfloat16)


def draw_prefix_len(key, part):
    slice_id = jnp.arange(SLICES, dtype=jnp.int32)
    reach_keys = jnp.minimum(slice_id * ROWS, LMAX)
    drawn = jax.random.randint(jax.random.fold_in(key, 17), (SLICES,), 0, reach_keys + 1, dtype=jnp.int32)
    return jnp.where(slice_id == SLICES - 1, LMAX, drawn).astype(jnp.int32)


def block_scale(own_key, dims, cuts, low, high):
    gain = 1.0
    for dim, shards_of in cuts:
        steps = jax.random.uniform(jax.random.fold_in(jax.random.fold_in(own_key, 6), dim), (shards_of,), jnp.float32, low / len(cuts), high / len(cuts))
        gain = gain * jnp.repeat(jnp.exp(steps), dims[dim] // shards_of).reshape((-1,) + (1,) * (len(dims) - 1 - dim))
    return gain


def noise(rng, dims, width, reach, split=(), kind=jnp.bfloat16):
    array = width * jax.random.normal(rng, dims, jnp.float32)
    if split:
        array = array * block_scale(rng, dims, split, -0.22, 0.18)
    return jnp.clip(array, -reach, reach).astype(kind)


def setup_inputs(seed: int = 0) -> dict:
    key_of = jax.random.split(jax.random.key(seed), 8)
    queries = draw_queries(jax.random.fold_in(key_of[7], 71), 0)
    keys = draw_keys(jax.random.fold_in(key_of[7], 71), 0)
    values = noise(key_of[2], (TOKENS, KV_HEADS * HEAD_DIM), 1.0, 6.0, ((0, 16), (1, 2)))
    d_attn = noise(key_of[3], (TOKENS, QHEADS * HEAD_DIM), 12.0, 72.0, ((0, 16), (1, 2)))
    d_out = noise(key_of[4], (TOKENS, D), 1.0, 6.0, ((0, 16), (1, 2)))
    w_query = noise(key_of[5], (D, QHEADS * HEAD_DIM), D ** -0.5, 0.09375, ((1, 2),))
    prefix_len = draw_prefix_len(jax.random.fold_in(key_of[7], 71), 0)
    return {"queries": queries, "keys": keys, "values": values, "d_attn": d_attn, "d_out": d_out, "w_query": w_query, "prefix_len": prefix_len}


masked_score = -1.0e30


def slice_gradient(slice_id, queries, keys, values, d_attn, d_out, w_query, prefix_len):
    window = LMAX + ROWS
    base_row = (slice_id * ROWS).astype(jnp.int32)
    window_start = jnp.maximum(base_row - LMAX, 0).astype(jnp.int32)
    lower_key = base_row - prefix_len[slice_id]
    positions = base_row + jnp.arange(ROWS, dtype=jnp.int32)
    key_position = window_start + jnp.arange(window, dtype=jnp.int32)
    allowed = (key_position[None, :] >= lower_key) & (key_position[None, :] <= positions[:, None])
    score_scale = HEAD_DIM ** -0.5
    group_width = QH_DEV * HEAD_DIM
    zero_index = jnp.int32(0)

    def add_group(group_index, running_total):
        group_index = group_index.astype(jnp.int32)
        column = (group_index * group_width).astype(jnp.int32)
        kv_column = (group_index * HEAD_DIM).astype(jnp.int32)
        query_block = lax.dynamic_slice(queries, (base_row, column), (ROWS, group_width))
        grad_block = lax.dynamic_slice(d_attn, (base_row, column), (ROWS, group_width))
        query_float = query_block.astype(jnp.float32).reshape(ROWS, QH_DEV, HEAD_DIM)
        grad_float = grad_block.astype(jnp.float32).reshape(ROWS, QH_DEV, HEAD_DIM)
        key_float = lax.dynamic_slice(keys, (window_start, kv_column), (window, HEAD_DIM)).astype(jnp.float32)
        value_float = lax.dynamic_slice(values, (window_start, kv_column), (window, HEAD_DIM)).astype(jnp.float32)
        scores = jnp.einsum("rjd,ud->jru", query_float, key_float, precision=lax.Precision.HIGHEST) * score_scale
        scores = jnp.where(allowed[None], scores, masked_score)
        row_max = jnp.max(scores, axis=2, keepdims=True)
        weights = jnp.where(allowed[None], jnp.exp(scores - row_max), 0.0)
        probability = weights / jnp.sum(weights, axis=2, keepdims=True)
        grad_prob = jnp.einsum("rjd,ud->jru", grad_float, value_float, precision=lax.Precision.HIGHEST)
        delta_rows = jnp.sum(probability * grad_prob, axis=2, keepdims=True)
        weighted_low = (probability * grad_prob).astype(jnp.bfloat16).astype(jnp.float32)
        probs_low = probability.astype(jnp.bfloat16).astype(jnp.float32)
        weighted_keys = jnp.einsum("jru,ud->jrd", weighted_low, key_float, precision=lax.Precision.HIGHEST)
        prob_keys = jnp.einsum("jru,ud->jrd", probs_low, key_float, precision=lax.Precision.HIGHEST)
        grad_query = (weighted_keys - delta_rows * prob_keys) * score_scale
        grad_query = grad_query.transpose(1, 0, 2).reshape(ROWS, group_width).astype(jnp.bfloat16)
        weight_block = lax.dynamic_slice(w_query, (zero_index, column), (D, group_width))
        partial_sum = lax.dot_general(grad_query, weight_block, (((1,), (1,)), ((), ())), preferred_element_type=jnp.float32)
        return running_total + partial_sum.astype(jnp.bfloat16).astype(jnp.float32)

    running_total = lax.fori_loop(0, KV_HEADS, add_group, jnp.zeros((ROWS, D), jnp.float32))
    own_out = lax.dynamic_slice(d_out, (base_row, zero_index), (ROWS, D))
    return (own_out.astype(jnp.float32) + running_total).astype(jnp.bfloat16)


def reference(queries, keys, values, d_attn, d_out, w_query, prefix_len):
    def one_slice(slice_id):
        return slice_gradient(slice_id, queries, keys, values, d_attn, d_out, w_query, prefix_len)

    hidden = lax.map(one_slice, jnp.arange(SLICES, dtype=jnp.int32))
    hidden = hidden.reshape(TOKENS, D)
    return jnp.concatenate([hidden[ROWS:], jnp.zeros((ROWS, D), jnp.bfloat16)], axis=0)
```

```python
import functools

import jax
import jax.numpy as jnp
from jax import lax
from jax.experimental import pallas as pl
from jax.experimental.pallas import tpu as pltpu
from jax.sharding import PartitionSpec as P

MESH = pl.DeviceIdType.MESH
masked_score = -1e30
log2_e = 1.4426950408889634
plane = 4
near_planes = 2
proj_tile = 512


def rows_by_rows(left, right):
    return lax.dot_general(
        left, right, (((1,), (1,)), ((), ())), preferred_element_type=jnp.float32
    )


def kernel(
    sections, heads, prefix_ref, q_ref, k_ref, v_ref, g_ref, dout_ref, w_ref, out_ref,
    kv, mine, gq, wbuf, din, run_max, run_sum, run_delta, total_grad, total_key,
    kv_recv, x_send, y_send, z_send, w_send, w_recv, w_local, d_send, d_recv,
    gq_send, gq_recv, fan_send, fan_recv,
):
    s = lax.axis_index("section")
    h = lax.axis_index("head")
    rows, head_width = k_ref.shape
    head_count = q_ref.shape[1] // head_width
    features = dout_ref.shape[1]
    planes = sections // plane
    z = s // plane
    p = s % plane
    x = p % 2
    y = p // 2
    px = p + 1 - 2 * x
    py = p + 2 - 4 * y
    pd = px + 2 - 4 * y
    x_side = z * plane + px
    y_side = z * plane + py

    def block(b):
        return kv.at[pl.ds(pl.multiple_of(b * rows, rows), rows), :]

    def kv_copy(b, target, sends):
        return pltpu.make_async_remote_copy(
            src_ref=block(b), dst_ref=block(b), send_sem=sends.at[b], recv_sem=kv_recv.at[b],
            device_id=(target, h), device_id_type=MESH,
        )

    def to_x(b):
        return kv_copy(b, x_side, x_send)

    def to_y(b):
        return kv_copy(b, y_side, y_send)

    def to_z(b):
        return kv_copy(b, s + plane, z_send)

    def arrive(b):
        to_x(b).wait_recv()

    barrier = pltpu.get_barrier_semaphore()

    def greet(section, head):
        pl.semaphore_signal(barrier, inc=1, device_id=(section, head), device_id_type=MESH)

    up = (z < planes - 1).astype(jnp.int32)
    down = (z > 0).astype(jnp.int32)
    after = (s < sections - 1).astype(jnp.int32)
    before = (s > 0).astype(jnp.int32)
    greet(x_side, h)
    greet(y_side, h)
    for step in range(1, heads):
        greet(s, (h + step) % heads)

    @pl.when(z < planes - 1)
    def _():
        greet(s + plane, h)

    @pl.when(z > 0)
    def _():
        greet(s - plane, h)

    @pl.when(s < sections - 1)
    def _():
        greet(s + 1, h)

    @pl.when(s > 0)
    def _():
        greet(s - 1, h)

    kv[pl.ds(pl.multiple_of(s * rows, rows), rows), :head_width] = k_ref[...]
    kv[pl.ds(pl.multiple_of(s * rows, rows), rows), head_width:] = v_ref[...]
    pl.semaphore_wait(barrier, 1 + heads + up + down + after + before)

    to_x(s).start()
    to_y(s).start()

    @pl.when(z < planes - 1)
    def _():
        to_z(s).start()

    def w_copy(step):
        peer = (h + step) % heads
        return pltpu.make_async_remote_copy(
            src_ref=w_ref.at[pl.ds(pl.multiple_of(peer * features, features), features), :],
            dst_ref=wbuf.at[h], send_sem=w_send.at[step], recv_sem=w_recv.at[step],
            device_id=(s, peer), device_id_type=MESH,
        )

    own_w = pltpu.make_async_copy(
        w_ref.at[pl.ds(pl.multiple_of(h * features, features), features), :], wbuf.at[h], w_local
    )

    def w_arrive(step):
        sender = (h + heads - step) % heads
        pltpu.make_async_remote_copy(
            src_ref=wbuf.at[sender], dst_ref=wbuf.at[sender],
            send_sem=w_send.at[step], recv_sem=w_recv.at[step],
            device_id=(s, sender), device_id_type=MESH,
        ).wait_recv()

    d_copy = pltpu.make_async_remote_copy(
        src_ref=dout_ref, dst_ref=din, send_sem=d_send, recv_sem=d_recv,
        device_id=(s - 1, h), device_id_type=MESH,
    )
    gq_copy = pltpu.make_async_remote_copy(
        src_ref=mine, dst_ref=gq.at[h], send_sem=gq_send, recv_sem=gq_recv,
        device_id=(s - 1, h), device_id_type=MESH,
    )

    lower = s * rows - prefix_ref[s]
    position = s * rows + lax.broadcasted_iota(jnp.int32, (rows, 1), 0)

    def attend(base, first):
        start = base * rows
        span = plane * rows
        keys = kv[pl.ds(pl.multiple_of(start, span), span), :head_width]
        values = kv[pl.ds(pl.multiple_of(start, span), span), head_width:]
        key_position = start + lax.broadcasted_iota(jnp.int32, (1, span), 1)
        allowed = key_position >= lower
        if first:
            allowed = allowed & (key_position <= position)
        for j in range(head_count):
            columns = slice(j * head_width, (j + 1) * head_width)
            scores = rows_by_rows(q_ref[:, columns], keys) * (head_width ** (-0.5) * log2_e)
            scores = jnp.where(allowed, scores, masked_score)
            top = jnp.max(scores, axis=1, keepdims=True)
            if not first:
                top = jnp.maximum(top, run_max[j])
                factor = jnp.exp2(run_max[j] - top)
            weights = jnp.exp2(scores - top)
            weighted = weights * rows_by_rows(g_ref[:, columns], values)
            part_sum = jnp.sum(weights, axis=1, keepdims=True)
            part_delta = jnp.sum(weighted, axis=1, keepdims=True)
            part_grad = jnp.dot(
                weighted.astype(jnp.bfloat16), keys, preferred_element_type=jnp.float32
            )
            part_key = jnp.dot(
                weights.astype(jnp.bfloat16), keys, preferred_element_type=jnp.float32
            )
            run_max[j] = top
            if first:
                run_sum[j] = part_sum
                run_delta[j] = part_delta
                total_grad[j] = part_grad
                total_key[j] = part_key
            else:
                run_sum[j] = run_sum[j] * factor + part_sum
                run_delta[j] = run_delta[j] * factor + part_delta
                total_grad[j] = total_grad[j] * factor + part_grad
                total_key[j] = total_key[j] * factor + part_key

    own = z * plane
    arrive(own + px)
    to_y(own + px).start()

    @pl.when(z < planes - 1)
    def _():
        to_z(own + px).start()

    @pl.when(s > 0)
    def _():
        d_copy.start()

    own_w.start()
    for step in range(1, heads):
        w_copy(step).start()
    arrive(own + py)

    def pass_far(distance, base):
        @pl.when((z < planes - 1) & (distance + 1 > near_planes))
        def _():
            to_z(base + py).start()
            to_z(base + pd).start()

    if near_planes == 0:
        @pl.when(z < planes - 1)
        def _():
            to_z(own + py).start()
    arrive(own + pd)
    if near_planes == 0:
        @pl.when(z < planes - 1)
        def _():
            to_z(own + pd).start()
    attend(own, True)

    def earlier_plane(distance, carry):
        base = (z - distance) * plane
        for column in (p, px):
            arrive(base + column)

            @pl.when(distance <= near_planes)
            def _():
                to_y(base + column).start()

            @pl.when(z < planes - 1)
            def _():
                to_z(base + column).start()

        arrive(base + py)
        arrive(base + pd)
        pass_far(distance, base)
        attend(base, False)
        return carry

    lax.fori_loop(1, z + 1, earlier_plane, 0)

    for j in range(head_count):
        inverse = 1.0 / run_sum[j]
        delta = run_delta[j] * inverse
        grad = (total_grad[j] - delta * total_key[j]) * (inverse * head_width ** (-0.5))
        mine[:, j * head_width:(j + 1) * head_width] = grad.astype(jnp.bfloat16)

    @pl.when(s > 0)
    def _():
        gq_copy.start()

    def fan_copy(step):
        return pltpu.make_async_remote_copy(
            src_ref=gq.at[h], dst_ref=gq.at[h], send_sem=fan_send.at[step],
            recv_sem=fan_recv.at[step], device_id=(s, (h + step) % heads), device_id_type=MESH,
        )

    def fan_arrive(step):
        sender = (h + heads - step) % heads
        pltpu.make_async_remote_copy(
            src_ref=gq.at[sender], dst_ref=gq.at[sender], send_sem=fan_send.at[step],
            recv_sem=fan_recv.at[step], device_id=(s, sender), device_id_type=MESH,
        ).wait_recv()

    own_w.wait()
    for step in range(1, heads):
        w_arrive(step)

    @pl.when(s < sections - 1)
    def _():
        gq_copy.wait_recv()
        for step in range(1, heads):
            fan_copy(step).start()
        d_copy.wait_recv()
        for step in range(1, heads):
            fan_arrive(step)
        tile = min(proj_tile, features)
        for t in range(features // tile):
            columns = slice(t * tile, (t + 1) * tile)
            hidden = din[:, columns].astype(jnp.float32)
            for group in range(heads):
                hidden = hidden + rows_by_rows(gq[group], wbuf[group, columns, :])
            out_ref[:, columns] = hidden.astype(jnp.bfloat16)
        for step in range(1, heads):
            fan_copy(step).wait_send()

    @pl.when(s == sections - 1)
    def _():
        out_ref[...] = jnp.zeros_like(out_ref)

    @pl.when(s > 0)
    def _():
        d_copy.wait_send()
        gq_copy.wait_send()

    for step in range(1, heads):
        w_copy(step).wait_send()
    to_x(s).wait_send()
    to_y(s).wait_send()
    to_y(own + px).wait_send()

    @pl.when(z < planes - 1)
    def _():
        to_z(s).wait_send()
        to_z(own + px).wait_send()
        if near_planes == 0:
            to_z(own + py).wait_send()
            to_z(own + pd).wait_send()

    def drain(distance, carry):
        base = (z - distance) * plane
        for column in (p, px):
            @pl.when(distance <= near_planes)
            def _():
                to_y(base + column).wait_send()

            @pl.when(z < planes - 1)
            def _():
                to_z(base + column).wait_send()

        @pl.when((z < planes - 1) & (distance + 1 > near_planes))
        def _():
            to_z(base + py).wait_send()
            to_z(base + pd).wait_send()

        return carry

    lax.fori_loop(1, z + 1, drain, 0)


def shards(queries, keys, values, d_attn, d_out, w_query, prefix_len):
    sections = lax.axis_size("section")
    heads = lax.axis_size("head")
    rows, head_width = keys.shape
    width = queries.shape[1]
    head_count = width // head_width
    features = d_out.shape[1]
    vmem = pl.BlockSpec(memory_space=pltpu.VMEM)
    anywhere = pl.BlockSpec(memory_space=pl.ANY)
    dma = pltpu.SemaphoreType.DMA
    return pl.pallas_call(
        functools.partial(kernel, sections, heads),
        out_shape=jax.ShapeDtypeStruct(d_out.shape, d_out.dtype),
        in_specs=[
            pl.BlockSpec(memory_space=pltpu.SMEM), vmem, vmem, vmem, vmem, anywhere, anywhere,
        ],
        out_specs=vmem,
        scratch_shapes=[
            pltpu.VMEM((sections * rows, 2 * head_width), jnp.bfloat16),
            pltpu.VMEM((rows, width), jnp.bfloat16),
            pltpu.VMEM((heads, rows, width), jnp.bfloat16),
            pltpu.VMEM((heads, features, width), jnp.bfloat16),
            pltpu.VMEM((rows, features), jnp.bfloat16),
            pltpu.VMEM((head_count, rows, 1), jnp.float32),
            pltpu.VMEM((head_count, rows, 1), jnp.float32),
            pltpu.VMEM((head_count, rows, 1), jnp.float32),
            pltpu.VMEM((head_count, rows, head_width), jnp.float32),
            pltpu.VMEM((head_count, rows, head_width), jnp.float32),
            dma((sections,)),
            dma((sections,)),
            dma((sections,)),
            dma((sections,)),
            dma((heads,)),
            dma((heads,)),
            dma,
            dma,
            dma,
            dma,
            dma,
            dma((heads,)),
            dma((heads,)),
        ],
        compiler_params=pltpu.CompilerParams(
            collective_id=0, has_side_effects=True, vmem_limit_bytes=40 * 1024 * 1024
        ),
    )(prefix_len, queries, keys, values, d_attn, d_out, w_query)


def solution(mesh):
    placed = (
        P("section", "head"),
        P("section", "head"),
        P("section", "head"),
        P("section", "head"),
        P("section", "head"),
        P(None, "head"),
        P(),
    )
    return jax.shard_map(
        shards, mesh=mesh, in_specs=placed, out_specs=P("section", "head"), check_vma=False
    )
```

```python
import functools

import jax
import jax.numpy as jnp
from jax import lax
from jax.experimental import pallas as pl
from jax.experimental.pallas import tpu as pltpu
from jax.sharding import PartitionSpec as P

MESH = pl.DeviceIdType.MESH
masked_score = -1e30
log2_e = 1.4426950408889634
plane = 4
near_left = 2
near_right = 0
proj_tile = 512


def rows_by_rows(left, right):
    return lax.dot_general(
        left, right, (((1,), (1,)), ((), ())), preferred_element_type=jnp.float32
    )


def kernel(
    sections, heads, prefix_ref, q_hbm, k_ref, v_ref, g_hbm, dout_ref, w_ref, out_ref,
    q_ref, g_ref, local_sem, partial, out_block, out_sem, kv, mine, gq, wbuf, din, run_max, run_sum, run_delta, total_grad, total_key,
    kv_recv, x_send, y_send, z_send, w_send, w_recv, w_local, d_send, d_recv,
    gq_send, gq_recv, fan_send, fan_recv,
):
    s = lax.axis_index("section")
    h = lax.axis_index("head")
    rows, head_width = k_ref.shape
    head_count = q_hbm.shape[1] // head_width
    features = dout_ref.shape[1]
    planes = sections // plane
    z = s // plane
    p = s % plane
    x = p % 2
    y = p // 2
    px = p + 1 - 2 * x
    py = p + 2 - 4 * y
    pd = px + 2 - 4 * y
    x_side = z * plane + px
    near = near_left * (1 - x) + near_right * x
    y_side = z * plane + py

    def block(b):
        return kv.at[pl.ds(pl.multiple_of(b * rows, rows), rows), :]

    def kv_copy(b, target, sends):
        return pltpu.make_async_remote_copy(
            src_ref=block(b), dst_ref=block(b), send_sem=sends.at[b], recv_sem=kv_recv.at[b],
            device_id=(target, h), device_id_type=MESH,
        )

    def to_x(b):
        return kv_copy(b, x_side, x_send)

    def to_y(b):
        return kv_copy(b, y_side, y_send)

    def to_z(b):
        return kv_copy(b, s + plane, z_send)

    def arrive(b):
        to_x(b).wait_recv()

    barrier = pltpu.get_barrier_semaphore()

    def greet(section, head):
        pl.semaphore_signal(barrier, inc=1, device_id=(section, head), device_id_type=MESH)

    up = (z < planes - 1).astype(jnp.int32)
    down = (z > 0).astype(jnp.int32)
    after = (s < sections - 1).astype(jnp.int32)
    before = (s > 0).astype(jnp.int32)
    greet(x_side, h)
    greet(y_side, h)
    for step in range(1, heads):
        greet(s, (h + step) % heads)

    @pl.when(z < planes - 1)
    def _():
        greet(s + plane, h)

    @pl.when(z > 0)
    def _():
        greet(s - plane, h)

    @pl.when(s < sections - 1)
    def _():
        greet(s + 1, h)

    @pl.when(s > 0)
    def _():
        greet(s - 1, h)

    own_rows = pl.ds(pl.multiple_of(s * rows, rows), rows)
    loads = [
        pltpu.make_async_copy(k_ref, kv.at[own_rows, :head_width], local_sem.at[0]),
        pltpu.make_async_copy(v_ref, kv.at[own_rows, head_width:], local_sem.at[1]),
        pltpu.make_async_copy(q_hbm, q_ref, local_sem.at[2]),
        pltpu.make_async_copy(g_hbm, g_ref, local_sem.at[3]),
    ]
    for load in loads:
        load.start()
    loads[0].wait()
    loads[1].wait()
    pl.semaphore_wait(barrier, 1 + heads + up + down + after + before)

    to_x(s).start()
    to_y(s).start()

    @pl.when(z < planes - 1)
    def _():
        to_z(s).start()

    def w_copy(step):
        peer = (h + step) % heads
        return pltpu.make_async_remote_copy(
            src_ref=w_ref.at[pl.ds(pl.multiple_of(peer * features, features), features), :],
            dst_ref=wbuf.at[h], send_sem=w_send.at[step], recv_sem=w_recv.at[step],
            device_id=(s, peer), device_id_type=MESH,
        )

    own_w = pltpu.make_async_copy(
        w_ref.at[pl.ds(pl.multiple_of(h * features, features), features), :], wbuf.at[h], w_local
    )

    def w_arrive(step):
        sender = (h + heads - step) % heads
        pltpu.make_async_remote_copy(
            src_ref=wbuf.at[sender], dst_ref=wbuf.at[sender],
            send_sem=w_send.at[step], recv_sem=w_recv.at[step],
            device_id=(s, sender), device_id_type=MESH,
        ).wait_recv()

    d_copy = pltpu.make_async_remote_copy(
        src_ref=dout_ref, dst_ref=din, send_sem=d_send, recv_sem=d_recv,
        device_id=(s - 1, h), device_id_type=MESH,
    )

    def gq_copy(j):
        return pltpu.make_async_remote_copy(
            src_ref=mine.at[j], dst_ref=gq.at[h, j], send_sem=gq_send.at[j],
            recv_sem=gq_recv.at[j], device_id=(s - 1, h), device_id_type=MESH,
        )

    def finish(j):
        inverse = 1.0 / run_sum[j]
        delta = run_delta[j] * inverse
        grad = (total_grad[j] - delta * total_key[j]) * (inverse * head_width ** (-0.5))
        mine[j] = grad.astype(jnp.bfloat16)

    lower = s * rows - prefix_ref[s]
    position = s * rows + lax.broadcasted_iota(jnp.int32, (rows, 1), 0)

    def attend(base, first, last=False):
        start = base * rows
        span = plane * rows
        keys = kv[pl.ds(pl.multiple_of(start, span), span), :head_width]
        values = kv[pl.ds(pl.multiple_of(start, span), span), head_width:]
        key_position = start + lax.broadcasted_iota(jnp.int32, (1, span), 1)
        allowed = key_position >= lower
        if first:
            allowed = allowed & (key_position <= position)
        for j in range(head_count):
            columns = slice(j * head_width, (j + 1) * head_width)
            scores = rows_by_rows(q_ref[:, columns], keys) * (head_width ** (-0.5) * log2_e)
            scores = jnp.where(allowed, scores, masked_score)
            top = jnp.max(scores, axis=1, keepdims=True)
            if not first:
                top = jnp.maximum(top, run_max[j])
                factor = jnp.exp2(run_max[j] - top)
            weights = jnp.exp2(scores - top)
            weighted = weights * rows_by_rows(g_ref[:, columns], values)
            part_sum = jnp.sum(weights, axis=1, keepdims=True)
            part_delta = jnp.sum(weighted, axis=1, keepdims=True)
            part_grad = jnp.dot(
                weighted.astype(jnp.bfloat16), keys, preferred_element_type=jnp.float32
            )
            part_key = jnp.dot(
                weights.astype(jnp.bfloat16), keys, preferred_element_type=jnp.float32
            )
            run_max[j] = top
            if first:
                run_sum[j] = part_sum
                run_delta[j] = part_delta
                total_grad[j] = part_grad
                total_key[j] = part_key
            else:
                run_sum[j] = run_sum[j] * factor + part_sum
                run_delta[j] = run_delta[j] * factor + part_delta
                total_grad[j] = total_grad[j] * factor + part_grad
                total_key[j] = total_key[j] * factor + part_key
            if last:
                finish(j)
                gq_copy(j).start()

    own = z * plane
    arrive(own + px)
    to_y(own + px).start()

    @pl.when(z < planes - 1)
    def _():
        to_z(own + px).start()

    own_w.start()
    for step in range(1, heads):
        w_copy(step).start()
    arrive(own + py)

    def pass_far(distance, base):
        @pl.when((z < planes - 1) & (distance + 1 > near))
        def _():
            to_z(base + py).start()
            to_z(base + pd).start()

    arrive(own + pd)
    pass_far(0, own)

    @pl.when(s > 0)
    def _():
        d_copy.start()

    loads[2].wait()
    loads[3].wait()
    attend(own, True)

    def earlier_plane(distance):
        base = (z - distance) * plane
        for column in (p, px):
            arrive(base + column)

            @pl.when(distance <= near)
            def _():
                to_y(base + column).start()

            @pl.when(z < planes - 1)
            def _():
                to_z(base + column).start()

        arrive(base + py)
        arrive(base + pd)
        pass_far(distance, base)

    def middle_plane(distance, carry):
        earlier_plane(distance)
        attend((z - distance) * plane, False)
        return carry

    lax.fori_loop(1, z, middle_plane, 0)

    @pl.when(z > 0)
    def _():
        earlier_plane(z)
        attend(0, False, True)

    @pl.when(z == 0)
    def _():
        for j in range(head_count):
            finish(j)

    @pl.when((z == 0) & (s > 0))
    def _():
        for j in range(head_count):
            gq_copy(j).start()

    def fan_copy(step, j):
        return pltpu.make_async_remote_copy(
            src_ref=gq.at[h, j], dst_ref=gq.at[h, j], send_sem=fan_send.at[step, j],
            recv_sem=fan_recv.at[step, j], device_id=(s, (h + step) % heads), device_id_type=MESH,
        )

    def fan_arrive(step, j):
        sender = (h + heads - step) % heads
        pltpu.make_async_remote_copy(
            src_ref=gq.at[sender, j], dst_ref=gq.at[sender, j], send_sem=fan_send.at[step, j],
            recv_sem=fan_recv.at[step, j], device_id=(s, sender), device_id_type=MESH,
        ).wait_recv()

    own_w.wait()
    for step in range(1, heads):
        w_arrive(step)

    tile = min(proj_tile, features)
    tiles = [slice(t * tile, (t + 1) * tile) for t in range(features // tile)]

    def out_copy(t):
        return pltpu.make_async_copy(out_block.at[:, tiles[t]], out_ref.at[:, tiles[t]], out_sem.at[t])

    @pl.when(s < sections - 1)
    def _():
        cut = max(head_count // 2, 1)
        parts = [range(i, min(i + cut, head_count)) for i in range(0, head_count, cut)]
        for index, part in enumerate(parts):
            for j in part:
                gq_copy(j).wait_recv()
                for step in range(1, heads):
                    fan_copy(step, j).start()
            if index == 0:
                d_copy.wait_recv()
            for j in part:
                for step in range(1, heads):
                    fan_arrive(step, j)
            channels = slice(part[0] * head_width, (part[-1] + 1) * head_width)
            grads = [
                jnp.concatenate([gq[group, j] for j in part], axis=1) for group in range(heads)
            ]
            for t, columns in enumerate(tiles):
                if index == 0:
                    hidden = din[:, columns].astype(jnp.float32)
                else:
                    hidden = partial[:, columns]
                for group in range(heads):
                    hidden = hidden + rows_by_rows(grads[group], wbuf[group, columns, channels])
                if index < len(parts) - 1:
                    partial[:, columns] = hidden
                else:
                    out_block[:, columns] = hidden.astype(jnp.bfloat16)
                    out_copy(t).start()
        for j in range(head_count):
            for step in range(1, heads):
                fan_copy(step, j).wait_send()

    @pl.when(s == sections - 1)
    def _():
        out_block[...] = jnp.zeros_like(out_block)
        for t in range(len(tiles)):
            out_copy(t).start()

    for t in range(len(tiles)):
        out_copy(t).wait()

    @pl.when(s > 0)
    def _():
        d_copy.wait_send()
        for j in range(head_count):
            gq_copy(j).wait_send()

    for step in range(1, heads):
        w_copy(step).wait_send()
    to_x(s).wait_send()
    to_y(s).wait_send()
    to_y(own + px).wait_send()

    @pl.when(z < planes - 1)
    def _():
        to_z(s).wait_send()
        to_z(own + px).wait_send()

    @pl.when((z < planes - 1) & (near < 1))
    def _():
        to_z(own + py).wait_send()
        to_z(own + pd).wait_send()

    def drain(distance, carry):
        base = (z - distance) * plane
        for column in (p, px):
            @pl.when(distance <= near)
            def _():
                to_y(base + column).wait_send()

            @pl.when(z < planes - 1)
            def _():
                to_z(base + column).wait_send()

        @pl.when((z < planes - 1) & (distance + 1 > near))
        def _():
            to_z(base + py).wait_send()
            to_z(base + pd).wait_send()

        return carry

    lax.fori_loop(1, z + 1, drain, 0)


def shards(queries, keys, values, d_attn, d_out, w_query, prefix_len):
    sections = lax.axis_size("section")
    heads = lax.axis_size("head")
    rows, head_width = keys.shape
    width = queries.shape[1]
    head_count = width // head_width
    features = d_out.shape[1]
    anywhere = pl.BlockSpec(memory_space=pl.ANY)
    dma = pltpu.SemaphoreType.DMA
    return pl.pallas_call(
        functools.partial(kernel, sections, heads),
        out_shape=jax.ShapeDtypeStruct(d_out.shape, d_out.dtype),
        in_specs=[
            pl.BlockSpec(memory_space=pltpu.SMEM), anywhere, anywhere, anywhere, anywhere,
            anywhere, anywhere,
        ],
        out_specs=anywhere,
        scratch_shapes=[
            pltpu.VMEM((rows, width), jnp.bfloat16),
            pltpu.VMEM((rows, width), jnp.bfloat16),
            dma((4,)),
            pltpu.VMEM((rows, features), jnp.float32),
            pltpu.VMEM((rows, features), jnp.bfloat16),
            dma((max(1, features // min(proj_tile, features)),)),
            pltpu.VMEM((sections * rows, 2 * head_width), jnp.bfloat16),
            pltpu.VMEM((head_count, rows, head_width), jnp.bfloat16),
            pltpu.VMEM((heads, head_count, rows, head_width), jnp.bfloat16),
            pltpu.VMEM((heads, features, width), jnp.bfloat16),
            pltpu.VMEM((rows, features), jnp.bfloat16),
            pltpu.VMEM((head_count, rows, 1), jnp.float32),
            pltpu.VMEM((head_count, rows, 1), jnp.float32),
            pltpu.VMEM((head_count, rows, 1), jnp.float32),
            pltpu.VMEM((head_count, rows, head_width), jnp.float32),
            pltpu.VMEM((head_count, rows, head_width), jnp.float32),
            dma((sections,)),
            dma((sections,)),
            dma((sections,)),
            dma((sections,)),
            dma((heads,)),
            dma((heads,)),
            dma,
            dma,
            dma,
            dma((head_count,)),
            dma((head_count,)),
            dma((heads, head_count)),
            dma((heads, head_count)),
        ],
        compiler_params=pltpu.CompilerParams(
            collective_id=0, has_side_effects=True, vmem_limit_bytes=62 * 1024 * 1024
        ),
    )(prefix_len, queries, keys, values, d_attn, d_out, w_query)


def solution(mesh):
    placed = (
        P("section", "head"),
        P("section", "head"),
        P("section", "head"),
        P("section", "head"),
        P("section", "head"),
        P(None, "head"),
        P(),
    )
    return jax.shard_map(
        shards, mesh=mesh, in_specs=placed, out_specs=P("section", "head"), check_vma=False
    )
```
